512 devices in a mesh: box: 128 (over z_hi, y, x), freq: 4 (over z_lo, core).
Axes of the slice: x: 4, y: 8, z: 8 (z_hi: 4, z_lo: 2; z = z_hi * 2 + z_lo), core: 2. Of those that a mesh axis runs over, the one named last changes fastest.
Arguments:
- currents: bfloat16 [4, 512, 2, 65536], P(None, 'freq', None, 'box'), may hold values from -6 to 6
- near_kernel: bfloat16 [4, 2, 98304, 512], P('freq', None, 'box'), may hold values from -0.15625 to 0.15625
- project_basis: bfloat16 [4, 2, 65536, 128], P('freq', None, 'box'), may hold values from -0.1875 to 0.1875
- level_self: bfloat16 [7, 4, 2, 16384, 128], P(None, 'freq', None, 'box'), may hold values from -0.25 to 0.25
- level_partner: bfloat16 [7, 4, 2, 16384, 128], P(None, 'freq', None, 'box'), may hold values from -0.25 to 0.25
- expand_basis: bfloat16 [4, 2, 16384, 512], P('freq', None, 'box'), may hold values from -0.375 to 0.375
Outputs:
- voltages: bfloat16 [4, 512, 2, 65536], P(None, 'freq', None, 'box')
The draws below stay inside these ranges and needn't reach their ends.
All inputs are finite; a program needn't handle non-finite values.
Results may differ from the reference program's by a relative error of at most 0.015.
Values may be sent and summed in bfloat16 or wider, within the bound.
A program may use at most 64 MiB of HBM per device.

```python
import jax
import jax.numpy as jnp
import numpy as np
from jax import lax

P_DEV = 512
HALO = 128
R = 128
SCEN = 512
FREQS = 4
BOXES = 128
PORTS = 65536
LEVELS = 7
N_BOX = 128


def shard_levels(stream_key, extent, shards, smallest, top_value):
    loudness, own = 1.0, jax.random.fold_in(stream_key, 6)
    for axis_at, blocks in shards:
        steps = jnp.exp(jax.random.uniform(jax.random.fold_in(own, axis_at), (blocks,), jnp.float32, smallest / len(shards), top_value / len(shards)))
        loudness = loudness * jnp.repeat(steps, extent[axis_at] // blocks).reshape([-1 if axis == axis_at else 1 for axis in range(len(extent))])
    return loudness


def normal_values(key, shape, scale, bound, pieces=(), held_as=jnp.bfloat16):
    level = shard_levels(key, shape, pieces, -0.22, 0.18) if pieces else 1.0
    values = jax.random.normal(key, shape, jnp.float32) * scale * level
    return jnp.minimum(jnp.maximum(values, -bound), bound).astype(held_as)


def setup_inputs(seed: int = 0) -> dict:
    key_list = jax.random.split(jax.random.key(seed), 7)
    currents = normal_values(key_list[0], (FREQS, SCEN, 2, PORTS), 1.0, 6.0, ((1, 4), (3, 128)))
    near_kernel = normal_values(key_list[1], (FREQS, 2, BOXES * (P_DEV + 2 * HALO), P_DEV), (2 * (P_DEV + 2 * HALO)) ** -0.5, 0.15625, ((0, 4), (2, 128)))
    project_basis = normal_values(key_list[2], (FREQS, 2, PORTS, R), (2 * P_DEV) ** -0.5, 0.1875, ((0, 4), (2, 128)))
    level_self = normal_values(key_list[3], (LEVELS, FREQS, 2, BOXES * R, R), (4 * R) ** -0.5, 0.25, ((1, 4), (3, 128)))
    level_partner = normal_values(key_list[4], (LEVELS, FREQS, 2, BOXES * R, R), (4 * R) ** -0.5, 0.25, ((1, 4), (3, 128)))
    expand_basis = normal_values(key_list[5], (FREQS, 2, BOXES * R, P_DEV), (2 * R) ** -0.5, 0.375, ((0, 4), (2, 128)))
    return dict(currents=currents, near_kernel=near_kernel, project_basis=project_basis, level_self=level_self, level_partner=level_partner, expand_basis=expand_basis)


def complex_block(real_part, imag_part):
    top_rows = jnp.concatenate([real_part, imag_part], axis=-1)
    bottom_rows = jnp.concatenate([-imag_part, real_part], axis=-1)
    return jnp.concatenate([top_rows, bottom_rows], axis=-2)


def reference(currents, near_kernel, project_basis, level_self, level_partner, expand_basis):
    box_total = N_BOX
    width = P_DEV + 2 * HALO
    results = []
    for freq_bin in range(FREQS):
        spectra = currents[freq_bin]
        by_box = jnp.transpose(spectra.reshape(SCEN, 2, box_total, P_DEV), (2, 0, 1, 3)).reshape(box_total, SCEN, 2 * P_DEV)
        project_inward = complex_block(project_basis[freq_bin, 0].reshape(box_total, P_DEV, R), project_basis[freq_bin, 1].reshape(box_total, P_DEV, R))
        series_weights = jnp.einsum("bsk,bkr->bsr", by_box.astype(jnp.float32), project_inward.astype(jnp.float32)).astype(jnp.bfloat16)
        for level_index in range(LEVELS):
            partner_index = np.arange(box_total) ^ (1 << level_index)
            partner = series_weights[partner_index]
            own_block = complex_block(level_self[level_index, freq_bin, 0].reshape(box_total, R, R), level_self[level_index, freq_bin, 1].reshape(box_total, R, R))
            other_block = complex_block(level_partner[level_index, freq_bin, 0].reshape(box_total, R, R), level_partner[level_index, freq_bin, 1].reshape(box_total, R, R))
            summed = jnp.einsum("bsk,bkr->bsr", series_weights.astype(jnp.float32), own_block.astype(jnp.float32))
            summed = summed + jnp.einsum("bsk,bkr->bsr", partner.astype(jnp.float32), other_block.astype(jnp.float32))
            series_weights = summed.astype(jnp.bfloat16)
        expand_outward = complex_block(expand_basis[freq_bin, 0].reshape(box_total, R, P_DEV), expand_basis[freq_bin, 1].reshape(box_total, R, P_DEV))
        distant_field = jnp.einsum("bsr,brk->bsk", series_weights.astype(jnp.float32), expand_outward.astype(jnp.float32))
        padded = jnp.pad(spectra, ((0, 0), (0, 0), (HALO, HALO)))
        near_real = near_kernel[freq_bin, 0].reshape(box_total, width, P_DEV)
        near_imag = near_kernel[freq_bin, 1].reshape(box_total, width, P_DEV)

        def near_box(entries):
            box_index, kernel_re, kernel_im = entries
            window = lax.dynamic_slice_in_dim(padded, box_index * P_DEV, width, 2).reshape(SCEN, 2 * width)
            return jnp.dot(window, complex_block(kernel_re, kernel_im), preferred_element_type=jnp.float32)

        near_field = lax.map(near_box, (jnp.arange(box_total, dtype=jnp.int32), near_real, near_imag))
        voltage = (distant_field + near_field).astype(jnp.bfloat16).reshape(box_total, SCEN, 2, P_DEV)
        results.append(jnp.transpose(voltage, (1, 2, 0, 3)).reshape(SCEN, 2, box_total * P_DEV))
    return jnp.stack(results)
```

```python
import functools

import jax
import jax.numpy as jnp
from jax import lax
from jax.experimental import pallas as pl
from jax.experimental.pallas import tpu as pltpu
from jax.sharding import PartitionSpec as P

HALO = 128
SUB = 2
MESH = pl.DeviceIdType.MESH
STAGES = ((0, 1), (2,), (3, 4), (5, 6))
STEPS = (
    ("project", 0, 0), ("project", 0, 1), ("rims", 0), ("project", 1, 0),
    ("project", 1, 1), ("level", 0, 0, 0), ("rims", 1), ("project", 2, 0),
    ("onward",), ("level", 0, 0, 1), ("project", 3, 0), ("level", 0, 1, 0),
    ("level", 1, 0, 0), ("level", 0, 1, 1), ("level", 1, 0, 1), ("project", 2, 1),
    ("rims", 2), ("level", 0, 2, 0), ("level", 1, 1, 0), ("level", 2, 0, 0),
    ("level", 0, 3, 0), ("project", 3, 1), ("level", 1, 1, 1), ("near", 0),
    ("rims", 3), ("level", 0, 2, 1), ("level", 2, 0, 1), ("level", 0, 3, 1),
    ("level", 1, 2, 0), ("level", 2, 1, 0), ("level", 3, 0, 0), ("near", 1),
    ("level", 1, 3, 0), ("level", 2, 1, 1), ("level", 3, 0, 1), ("level", 1, 2, 1),
    ("level", 2, 2, 0), ("finish", 0, 1), ("finish", 0, 0), ("level", 3, 1, 0),
    ("level", 2, 3, 0), ("level", 1, 3, 1), ("finish", 1, 0), ("level", 2, 2, 1),
    ("level", 3, 2, 0), ("finish", 2, 0), ("level", 2, 3, 1), ("level", 3, 3, 0),
    ("level", 3, 1, 1), ("finish", 3, 0), ("finish", 1, 1), ("level", 3, 2, 1),
    ("finish", 2, 1), ("level", 3, 3, 1), ("finish", 3, 1),
)


def flip(index, stride):
    return index + stride - 2 * stride * ((index // stride) % 2)


def kernel(
    cur, near, proj, own, other, expand, out,
    spec, low_rim, high_rim, near_re, near_im, near_neg, w_in, w_lev, w_out, far_raw, w_far, w_two, coef, part_in, near_sum, volt,
    load_sem, spec_sem, fwd_send, fwd_recv, rim_send, rim_recv, lev_send, lev_recv, far_send, far_recv, ret_send, ret_recv, home_sem,
):
    box, f = lax.axis_index("box"), lax.axis_index("freq")
    boxes = lax.axis_size("box")
    levels = own.shape[0]
    scen, ports = spec.shape[2], spec.shape[3]
    rank = proj.shape[-1]
    rows = scen // SUB
    up, down = lax.rem(box + 1, boxes), lax.rem(box + boxes - 1, boxes)
    peers = [f, flip(f, 1), flip(f, 2), flip(flip(f, 2), 1)]
    stages = len(STAGES)
    mates, pairs = [], []
    for stage in STAGES:
        first = flip(box, 1 << stage[0])
        if len(stage) == 2:
            mates.append([first, flip(box, 1 << stage[1]), flip(first, 1 << stage[1])])
            pairs.append(mates[-1][1])
        else:
            mates.append([first])
    everyone = [there for group in mates for there in group] + [up, down]

    barrier = pltpu.get_barrier_semaphore()
    for slot in (2, 3, 1):
        pl.semaphore_signal(barrier, inc=1, device_id={"freq": peers[slot]}, device_id_type=MESH)
    for there in everyone:
        pl.semaphore_signal(barrier, inc=1, device_id={"box": there}, device_id_type=MESH)

    own_copy = pltpu.make_async_copy(cur.at[f], spec.at[0], spec_sem)
    own_copy.start()
    loads = []

    def load(source, target):
        copy = pltpu.make_async_copy(source, target, load_sem.at[len(loads)])
        copy.start()
        loads.append(copy)

    load(proj.at[0, 0], w_in.at[0:ports, 0:rank])
    load(proj.at[0, 1], w_in.at[0:ports, rank : 2 * rank])
    load(proj.at[0, 0], w_in.at[ports : 2 * ports, rank : 2 * rank])
    for source, base in ((own, 0), (other, 2 * rank)):
        load(source.at[:, 0, 0], w_lev.at[:, base : base + rank, 0:rank])
        load(source.at[:, 0, 1], w_lev.at[:, base : base + rank, rank : 2 * rank])
        load(source.at[:, 0, 0], w_lev.at[:, base + rank : base + 2 * rank, rank : 2 * rank])
    load(near.at[0, 0], near_re)
    load(near.at[0, 1], near_im)
    load(expand.at[0, 0], w_out.at[0:rank, 0:ports])
    load(expand.at[0, 1], w_out.at[0:rank, ports : 2 * ports])
    load(expand.at[0, 0], w_out.at[rank : 2 * rank, ports : 2 * ports])

    pl.semaphore_wait(barrier, 3 + len(everyone))

    def forward(slot, part):
        lines = pl.ds(part * rows, rows)
        return pltpu.make_async_remote_copy(
            src_ref=cur.at[peers[slot], :, lines],
            dst_ref=spec.at[slot, :, lines],
            send_sem=fwd_send.at[slot, part],
            recv_sem=fwd_recv.at[slot, part],
            device_id={"freq": peers[slot]},
            device_id_type=MESH,
        )

    def rim(slot, side):
        columns = pl.ds(ports - HALO, HALO) if side == 0 else pl.ds(0, HALO)
        return pltpu.make_async_remote_copy(
            src_ref=spec.at[slot, :, :, columns],
            dst_ref=(low_rim, high_rim)[side].at[slot],
            send_sem=rim_send.at[side, slot],
            recv_sem=rim_recv.at[side, slot],
            device_id={"box": (up, down)[side]},
            device_id_type=MESH,
        )

    def exchange(stage, slot, part):
        lines = pl.ds(part * rows, rows)
        return [
            pltpu.make_async_remote_copy(
                src_ref=coef.at[stage, slot, lines],
                dst_ref=part_in.at[stage, place, slot, lines],
                send_sem=lev_send.at[stage, place, slot, part],
                recv_sem=lev_recv.at[stage, place, slot, part],
                device_id={"box": there},
                device_id_type=MESH,
            )
            for place, there in enumerate(mates[stage])
        ]

    twos = [stage for stage in range(stages) if len(STAGES[stage]) == 2]

    def factors(place):
        stage = STAGES[twos[place]]
        return [
            pltpu.make_async_remote_copy(
                src_ref=source.at[stage[0], 0],
                dst_ref=far_raw.at[place, which],
                send_sem=far_send.at[place, which],
                recv_sem=far_recv.at[place, which],
                device_id={"box": pairs[place]},
                device_id_type=MESH,
            )
            for which, source in enumerate((own, other))
        ]

    def give_back(slot, part):
        lines = pl.ds(part * rows, rows)
        return pltpu.make_async_remote_copy(
            src_ref=volt.at[slot, :, lines],
            dst_ref=out.at[f, :, lines],
            send_sem=ret_send.at[slot, part],
            recv_sem=ret_recv.at[slot, part],
            device_id={"freq": peers[slot]},
            device_id_type=MESH,
        )

    def arrive(slot, part):
        lines = pl.ds(part * rows, rows)
        return pltpu.make_async_remote_copy(
            src_ref=volt.at[slot, :, lines],
            dst_ref=out.at[peers[slot], :, lines],
            send_sem=ret_send.at[slot, part],
            recv_sem=ret_recv.at[slot, part],
            device_id={"freq": peers[slot]},
            device_id_type=MESH,
        )

    def home(part):
        lines = pl.ds(part * rows, rows)
        return pltpu.make_async_copy(volt.at[0, :, lines], out.at[f, :, lines], home_sem.at[part])

    for slot in (2, 3):
        forward(slot, 0).start()
    for part in range(SUB):
        forward(1, part).start()
    for place in range(len(twos)):
        for copy in factors(place):
            copy.start()

    def dot(left, right):
        return jnp.dot(left, right, preferred_element_type=jnp.float32)

    for copy in loads[:3]:
        copy.wait()
    w_in[ports : 2 * ports, 0:rank] = -w_in[0:ports, rank : 2 * rank]
    own_copy.wait()
    prepared = set()

    def prepare(what):
        if what in prepared:
            return
        prepared.add(what)
        if what == "level":
            for copy in loads[3:9]:
                copy.wait()
            for base in (0, 2 * rank):
                w_lev[:, base + rank : base + 2 * rank, 0:rank] = -w_lev[:, base : base + rank, rank : 2 * rank]
        elif isinstance(what, int):
            for copy in factors(what):
                copy.wait()
            low, high = STAGES[twos[what]]
            for which in range(2):
                top, real, imag = 2 * rank * which, far_raw[what, which, 0], far_raw[what, which, 1]
                w_far[top : top + rank, 0:rank] = real
                w_far[top : top + rank, rank : 2 * rank] = imag
                w_far[top + rank : top + 2 * rank, 0:rank] = -imag
                w_far[top + rank : top + 2 * rank, rank : 2 * rank] = real
            near_half = dot(w_lev[low], w_lev[high, 0 : 2 * rank])
            far_half = dot(w_far[...], w_lev[high, 2 * rank : 4 * rank])
            w_two[what, 0 : 4 * rank] = near_half.astype(jnp.bfloat16)
            w_two[what, 4 * rank : 8 * rank] = far_half.astype(jnp.bfloat16)
        elif what == "near":
            for copy in loads[9:11]:
                copy.wait()

            @pl.when(box == 0)
            def _():
                near_re[0:HALO] = jnp.zeros((HALO, ports), jnp.bfloat16)
                near_im[0:HALO] = jnp.zeros((HALO, ports), jnp.bfloat16)

            @pl.when(box == boxes - 1)
            def _():
                near_re[HALO + ports :] = jnp.zeros((HALO, ports), jnp.bfloat16)
                near_im[HALO + ports :] = jnp.zeros((HALO, ports), jnp.bfloat16)

            near_neg[...] = -near_im[...]
        else:
            for copy in loads[11:14]:
                copy.wait()
            w_out[rank : 2 * rank, 0:ports] = -w_out[0:rank, ports : 2 * ports]

    for step in STEPS:
        kind = step[0]
        if kind == "project":
            slot, part = step[1:]
            lines = pl.ds(part * rows, rows)
            if slot != 0:
                forward(slot, part).wait_recv()
            total = dot(spec[slot, 0, lines], w_in[0:ports]) + dot(spec[slot, 1, lines], w_in[ports : 2 * ports])
            coef[0, slot, lines] = total.astype(jnp.bfloat16)
            for copy in exchange(0, slot, part):
                copy.start()
            prepare("level")
        elif kind == "onward":
            for part in range(1, SUB):
                for slot in (2, 3):
                    forward(slot, part).start()
        elif kind == "rims":
            for side in range(2):
                rim(step[1], side).start()
        elif kind == "level":
            stage, slot, part = step[1:]
            lines = pl.ds(part * rows, rows)
            if stage in twos:
                prepare(twos.index(stage))
                weights = w_two.at[twos.index(stage)]
            else:
                weights = w_lev.at[STAGES[stage][0]]
            for copy in exchange(stage, slot, part):
                copy.wait_recv()
            blocks = [coef[stage, slot, lines]] + [part_in[stage, place, slot, lines] for place in range(len(mates[stage]))]
            total = dot(jnp.concatenate(blocks, axis=-1), weights[...])
            coef[stage + 1, slot, lines] = total.astype(jnp.bfloat16)
            if stage + 1 < stages:
                for copy in exchange(stage + 1, slot, part):
                    copy.start()
        elif kind == "near":
            prepare("near")
            prepare("out")
            pair = (2 * step[1], 2 * step[1] + 1)
            for slot in pair:
                for side in range(2):
                    rim(slot, side).wait_recv()

            def window(component):
                bands = [low_rim[pair[0] : pair[1] + 1, component], spec[pair[0] : pair[1] + 1, component], high_rim[pair[0] : pair[1] + 1, component]]
                return jnp.concatenate([band.reshape(2 * scen, band.shape[-1]) for band in bands], axis=-1)

            real, imag = window(0), window(1)
            near_sum[pair[0] : pair[1] + 1, :, 0:ports] = (dot(real, near_re[...]) + dot(imag, near_neg[...])).reshape(2, scen, ports)
            near_sum[pair[0] : pair[1] + 1, :, ports:] = (dot(real, near_im[...]) + dot(imag, near_re[...])).reshape(2, scen, ports)
        else:
            slot, part = step[1:]
            lines = pl.ds(part * rows, rows)
            total = (dot(coef[stages, slot, lines], w_out[...]) + near_sum[slot, lines]).astype(jnp.bfloat16)
            volt[slot, 0, lines] = total[:, 0:ports]
            volt[slot, 1, lines] = total[:, ports:]
            if slot == 0:
                home(part).start()
            else:
                give_back(slot, part).start()

    for slot in range(4):
        for side in range(2):
            rim(slot, side).wait_send()
        for part in range(SUB):
            for stage in range(stages):
                for copy in exchange(stage, slot, part):
                    copy.wait_send()
            if slot == 0:
                home(part).wait()
            else:
                forward(slot, part).wait_send()
                give_back(slot, part).wait_send()
                arrive(slot, part).wait_recv()


def local(currents, near_kernel, project_basis, level_self, level_partner, expand_basis):
    spectra = jnp.transpose(currents, (0, 2, 1, 3))
    bins, _, scen, ports = spectra.shape
    levels, rank = level_self.shape[0], level_self.shape[-1]
    width = near_kernel.shape[2]
    half = jnp.bfloat16
    stages, twos = len(STAGES), sum(len(stage) == 2 for stage in STAGES)
    voltages = pl.pallas_call(
        kernel,
        out_shape=jax.ShapeDtypeStruct(spectra.shape, half),
        in_specs=[pl.BlockSpec(memory_space=pl.ANY)] * 6,
        out_specs=pl.BlockSpec(memory_space=pl.ANY),
        scratch_shapes=[
            pltpu.VMEM((4, 2, scen, ports), half),
            pltpu.VMEM((4, 2, scen, HALO), half),
            pltpu.VMEM((4, 2, scen, HALO), half),
            pltpu.VMEM((width, ports), half),
            pltpu.VMEM((width, ports), half),
            pltpu.VMEM((width, ports), half),
            pltpu.VMEM((2 * ports, 2 * rank), half),
            pltpu.VMEM((levels, 4 * rank, 2 * rank), half),
            pltpu.VMEM((2 * rank, 2 * ports), half),
            pltpu.VMEM((max(twos, 1), 2, 2, rank, rank), half),
            pltpu.VMEM((4 * rank, 2 * rank), half),
            pltpu.VMEM((max(twos, 1), 8 * rank, 2 * rank), half),
            pltpu.VMEM((stages + 1, 4, scen, 2 * rank), half),
            pltpu.VMEM((stages, 3, 4, scen, 2 * rank), half),
            pltpu.VMEM((4, scen, 2 * ports), jnp.float32),
            pltpu.VMEM((4, 2, scen, ports), half),
            pltpu.SemaphoreType.DMA((14,)),
            pltpu.SemaphoreType.DMA,
            pltpu.SemaphoreType.DMA((4, SUB)),
            pltpu.SemaphoreType.DMA((4, SUB)),
            pltpu.SemaphoreType.DMA((2, 4)),
            pltpu.SemaphoreType.DMA((2, 4)),
            pltpu.SemaphoreType.DMA((stages, 3, 4, SUB)),
            pltpu.SemaphoreType.DMA((stages, 3, 4, SUB)),
            pltpu.SemaphoreType.DMA((max(twos, 1), 2)),
            pltpu.SemaphoreType.DMA((max(twos, 1), 2)),
            pltpu.SemaphoreType.DMA((4, SUB)),
            pltpu.SemaphoreType.DMA((4, SUB)),
            pltpu.SemaphoreType.DMA((SUB,)),
        ],
        compiler_params=pltpu.CompilerParams(collective_id=0, has_side_effects=True, vmem_limit_bytes=50 * 1024 * 1024),
        cost_estimate=pl.CostEstimate(flops=3 << 30, bytes_accessed=6 << 20, transcendentals=0),
    )(spectra, near_kernel, project_basis, level_self, level_partner, expand_basis)
    return jnp.transpose(voltages, (0, 2, 1, 3))


def solution(mesh):
    return jax.shard_map(
        local,
        mesh=mesh,
        in_specs=(
            P(None, "freq", None, "box"),
            P("freq", None, "box", None),
            P("freq", None, "box", None),
            P(None, "freq", None, "box", None),
            P(None, "freq", None, "box", None),
            P("freq", None, "box", None),
        ),
        out_specs=P(None, "freq", None, "box"),
        check_vma=False,
    )
```

```python
import functools

import jax
import jax.numpy as jnp
from jax import lax
from jax.experimental import pallas as pl
from jax.experimental.pallas import tpu as pltpu
from jax.sharding import PartitionSpec as P

HALO = 128
SUB = 1
MESH = pl.DeviceIdType.MESH
STAGES = ((0, 1), (2,), (3, 4), (5, 6))
STEPS = (
    ("project", 0, 0), ("project", 1, 0), ("rims", 0), ("level", 0, 0, 0),
    ("rims", 1), ("level", 0, 1, 0), ("project", 2, 0), ("level", 1, 0, 0),
    ("level", 0, 2, 0), ("project", 3, 0), ("level", 1, 1, 0), ("near", 0),
    ("level", 2, 0, 0), ("level", 0, 3, 0), ("rims", 2), ("rims", 3),
    ("level", 1, 2, 0), ("level", 2, 1, 0), ("level", 1, 3, 0), ("near", 1),
    ("level", 2, 2, 0), ("level", 2, 3, 0), ("level", 3, 2, 0), ("level", 3, 0, 0),
    ("finish", 2, 0), ("level", 3, 3, 0), ("finish", 3, 0), ("level", 3, 1, 0),
    ("finish", 0, 0), ("finish", 1, 0),
)


def flip(index, stride):
    return index + stride - 2 * stride * ((index // stride) % 2)


def kernel(
    cur, near, proj, own, other, expand, out,
    spec, low_rim, high_rim, near_re, near_im, near_neg, w_in, w_lev, w_out, far_raw, w_far, w_two, coef, part_in, near_sum, volt,
    load_sem, spec_sem, fwd_send, fwd_recv, rim_send, rim_recv, lev_send, lev_recv, far_send, far_recv, ret_send, ret_recv, home_sem,
):
    box, f = lax.axis_index("box"), lax.axis_index("freq")
    boxes = lax.axis_size("box")
    levels = own.shape[0]
    scen, ports = spec.shape[2], spec.shape[3]
    rank = proj.shape[-1]
    rows = scen // SUB
    up, down = lax.rem(box + 1, boxes), lax.rem(box + boxes - 1, boxes)
    peers = [f, flip(f, 1), flip(f, 2), flip(flip(f, 2), 1)]
    stages = len(STAGES)
    mates, pairs = [], []
    for stage in STAGES:
        first = flip(box, 1 << stage[0])
        if len(stage) == 2:
            mates.append([first, flip(box, 1 << stage[1]), flip(first, 1 << stage[1])])
            pairs.append(mates[-1][1])
        else:
            mates.append([first])
    everyone = [there for group in mates for there in group] + [up, down]

    barrier = pltpu.get_barrier_semaphore()
    for slot in (2, 3, 1):
        pl.semaphore_signal(barrier, inc=1, device_id={"freq": peers[slot]}, device_id_type=MESH)
    for there in everyone:
        pl.semaphore_signal(barrier, inc=1, device_id={"box": there}, device_id_type=MESH)

    own_copy = pltpu.make_async_copy(cur.at[f], spec.at[0], spec_sem)
    own_copy.start()
    loads = []

    def load(source, target):
        copy = pltpu.make_async_copy(source, target, load_sem.at[len(loads)])
        copy.start()
        loads.append(copy)

    load(proj.at[0, 0], w_in.at[0:ports, 0:rank])
    load(proj.at[0, 1], w_in.at[0:ports, rank : 2 * rank])
    load(proj.at[0, 0], w_in.at[ports : 2 * ports, rank : 2 * rank])
    for source, base in ((own, 0), (other, 2 * rank)):
        load(source.at[:, 0, 0], w_lev.at[:, base : base + rank, 0:rank])
        load(source.at[:, 0, 1], w_lev.at[:, base : base + rank, rank : 2 * rank])
        load(source.at[:, 0, 0], w_lev.at[:, base + rank : base + 2 * rank, rank : 2 * rank])
    load(near.at[0, 0], near_re)
    load(near.at[0, 1], near_im)
    load(expand.at[0, 0], w_out.at[0:rank, 0:ports])
    load(expand.at[0, 1], w_out.at[0:rank, ports : 2 * ports])
    load(expand.at[0, 0], w_out.at[rank : 2 * rank, ports : 2 * ports])

    pl.semaphore_wait(barrier, 3 + len(everyone))

    def forward(slot, part):
        lines = pl.ds(part * rows, rows)
        return pltpu.make_async_remote_copy(
            src_ref=cur.at[peers[slot], :, lines],
            dst_ref=spec.at[slot, :, lines],
            send_sem=fwd_send.at[slot],
            recv_sem=fwd_recv.at[slot, part],
            device_id={"freq": peers[slot]},
            device_id_type=MESH,
        )

    def rim(slot, side):
        columns = pl.ds(ports - HALO, HALO) if side == 0 else pl.ds(0, HALO)
        return pltpu.make_async_remote_copy(
            src_ref=spec.at[slot, :, :, columns],
            dst_ref=(low_rim, high_rim)[side].at[slot],
            send_sem=rim_send.at[side],
            recv_sem=rim_recv.at[side, slot],
            device_id={"box": (up, down)[side]},
            device_id_type=MESH,
        )

    def exchange(stage, slot, part):
        lines = pl.ds(part * rows, rows)
        return [
            pltpu.make_async_remote_copy(
                src_ref=coef.at[stage, slot, lines],
                dst_ref=part_in.at[stage, place, slot, lines],
                send_sem=lev_send.at[stage, place],
                recv_sem=lev_recv.at[stage, slot, part],
                device_id={"box": there},
                device_id_type=MESH,
            )
            for place, there in enumerate(mates[stage])
        ]

    def landed(stage, slot, part):
        block = part_in.at[stage, pl.ds(0, len(mates[stage])), slot, pl.ds(part * rows, rows)]
        return pltpu.make_async_copy(block, block, lev_recv.at[stage, slot, part])

    def drained(ref, sem):
        pltpu.make_async_copy(ref, ref, sem).wait()

    twos = [stage for stage in range(stages) if len(STAGES[stage]) == 2]

    def factors(place):
        stage = STAGES[twos[place]]
        return [
            pltpu.make_async_remote_copy(
                src_ref=source.at[stage[0], 0],
                dst_ref=far_raw.at[place, which],
                send_sem=far_send.at[place, which],
                recv_sem=far_recv.at[place, which],
                device_id={"box": pairs[place]},
                device_id_type=MESH,
            )
            for which, source in enumerate((own, other))
        ]

    def give_back(slot, part):
        lines = pl.ds(part * rows, rows)
        return pltpu.make_async_remote_copy(
            src_ref=volt.at[slot, :, lines],
            dst_ref=out.at[f, :, lines],
            send_sem=ret_send.at[slot],
            recv_sem=ret_recv.at[slot],
            device_id={"freq": peers[slot]},
            device_id_type=MESH,
        )

    def home(part):
        lines = pl.ds(part * rows, rows)
        return pltpu.make_async_copy(volt.at[0, :, lines], out.at[f, :, lines], home_sem)

    for slot in (2, 3):
        forward(slot, 0).start()
    for part in range(SUB):
        forward(1, part).start()
    for place in range(len(twos)):
        for copy in factors(place):
            copy.start()

    def dot(left, right):
        return jnp.dot(left, right, preferred_element_type=jnp.float32)

    for copy in loads[:3]:
        copy.wait()
    w_in[ports : 2 * ports, 0:rank] = -w_in[0:ports, rank : 2 * rank]
    own_copy.wait()
    prepared = set()

    def prepare(what):
        if what in prepared:
            return
        prepared.add(what)
        if what == "level":
            for copy in loads[3:9]:
                copy.wait()
            for base in (0, 2 * rank):
                w_lev[:, base + rank : base + 2 * rank, 0:rank] = -w_lev[:, base : base + rank, rank : 2 * rank]
        elif isinstance(what, int):
            for copy in factors(what):
                copy.wait()
            low, high = STAGES[twos[what]]
            for which in range(2):
                top, real, imag = 2 * rank * which, far_raw[what, which, 0], far_raw[what, which, 1]
                w_far[top : top + rank, 0:rank] = real
                w_far[top : top + rank, rank : 2 * rank] = imag
                w_far[top + rank : top + 2 * rank, 0:rank] = -imag
                w_far[top + rank : top + 2 * rank, rank : 2 * rank] = real
            near_half = dot(w_lev[low], w_lev[high, 0 : 2 * rank])
            far_half = dot(w_far[...], w_lev[high, 2 * rank : 4 * rank])
            w_two[what, 0 : 4 * rank] = near_half.astype(jnp.bfloat16)
            w_two[what, 4 * rank : 8 * rank] = far_half.astype(jnp.bfloat16)
        elif what == "near":
            for copy in loads[9:11]:
                copy.wait()

            @pl.when(box == 0)
            def _():
                near_re[0:HALO] = jnp.zeros((HALO, ports), jnp.bfloat16)
                near_im[0:HALO] = jnp.zeros((HALO, ports), jnp.bfloat16)

            @pl.when(box == boxes - 1)
            def _():
                near_re[HALO + ports :] = jnp.zeros((HALO, ports), jnp.bfloat16)
                near_im[HALO + ports :] = jnp.zeros((HALO, ports), jnp.bfloat16)

            near_neg[...] = -near_im[...]
        else:
            for copy in loads[11:14]:
                copy.wait()
            w_out[rank : 2 * rank, 0:ports] = -w_out[0:rank, ports : 2 * ports]

    for step in STEPS:
        kind = step[0]
        if kind == "project":
            slot, part = step[1:]
            lines = pl.ds(part * rows, rows)
            if slot != 0:
                forward(slot, part).wait_recv()
            total = dot(spec[slot, 0, lines], w_in[0:ports]) + dot(spec[slot, 1, lines], w_in[ports : 2 * ports])
            coef[0, slot, lines] = total.astype(jnp.bfloat16)
            for copy in exchange(0, slot, part):
                copy.start()
            prepare("level")
        elif kind == "onward":
            for part in range(1, SUB):
                for slot in (2, 3):
                    forward(slot, part).start()
        elif kind == "rims":
            for side in range(2):
                rim(step[1], side).start()
        elif kind == "level":
            stage, slot, part = step[1:]
            lines = pl.ds(part * rows, rows)
            if stage in twos:
                prepare(twos.index(stage))
                weights = w_two.at[twos.index(stage)]
            else:
                weights = w_lev.at[STAGES[stage][0]]
            landed(stage, slot, part).wait()
            blocks = [coef[stage, slot, lines]] + [part_in[stage, place, slot, lines] for place in range(len(mates[stage]))]
            total = dot(jnp.concatenate(blocks, axis=-1), weights[...])
            coef[stage + 1, slot, lines] = total.astype(jnp.bfloat16)
            if stage + 1 < stages:
                for copy in exchange(stage + 1, slot, part):
                    copy.start()
        elif kind == "near":
            prepare("near")
            prepare("out")
            pair = (2 * step[1], 2 * step[1] + 1)
            for slot in pair:
                for side in range(2):
                    rim(slot, side).wait_recv()

            def window(component):
                bands = [low_rim[pair[0] : pair[1] + 1, component], spec[pair[0] : pair[1] + 1, component], high_rim[pair[0] : pair[1] + 1, component]]
                return jnp.concatenate([band.reshape(2 * scen, band.shape[-1]) for band in bands], axis=-1)

            real, imag = window(0), window(1)
            near_sum[pair[0] : pair[1] + 1, :, 0:ports] = (dot(real, near_re[...]) + dot(imag, near_neg[...])).reshape(2, scen, ports)
            near_sum[pair[0] : pair[1] + 1, :, ports:] = (dot(real, near_im[...]) + dot(imag, near_re[...])).reshape(2, scen, ports)
        else:
            slot, part = step[1:]
            lines = pl.ds(part * rows, rows)
            total = (dot(coef[stages, slot, lines], w_out[...]) + near_sum[slot, lines]).astype(jnp.bfloat16)
            volt[slot, 0, lines] = total[:, 0:ports]
            volt[slot, 1, lines] = total[:, ports:]
            if slot == 0:
                home(part).start()
            else:
                give_back(slot, part).start()

    drained(low_rim, rim_send.at[0])
    drained(high_rim, rim_send.at[1])
    for stage in range(stages):
        for place in range(len(mates[stage])):
            drained(coef.at[stage], lev_send.at[stage, place])
    for slot in range(1, 4):
        drained(spec.at[slot], fwd_send.at[slot])
        drained(volt.at[slot], ret_send.at[slot])
        drained(out.at[peers[slot]], ret_recv.at[slot])
    drained(volt.at[0], home_sem)


def local(currents, near_kernel, project_basis, level_self, level_partner, expand_basis):
    spectra = jnp.transpose(currents, (0, 2, 1, 3))
    bins, _, scen, ports = spectra.shape
    levels, rank = level_self.shape[0], level_self.shape[-1]
    width = near_kernel.shape[2]
    half = jnp.bfloat16
    stages, twos = len(STAGES), sum(len(stage) == 2 for stage in STAGES)
    voltages = pl.pallas_call(
        kernel,
        out_shape=jax.ShapeDtypeStruct(spectra.shape, half),
        in_specs=[pl.BlockSpec(memory_space=pl.ANY)] * 6,
        out_specs=pl.BlockSpec(memory_space=pl.ANY),
        scratch_shapes=[
            pltpu.VMEM((4, 2, scen, ports), half),
            pltpu.VMEM((4, 2, scen, HALO), half),
            pltpu.VMEM((4, 2, scen, HALO), half),
            pltpu.VMEM((width, ports), half),
            pltpu.VMEM((width, ports), half),
            pltpu.VMEM((width, ports), half),
            pltpu.VMEM((2 * ports, 2 * rank), half),
            pltpu.VMEM((levels, 4 * rank, 2 * rank), half),
            pltpu.VMEM((2 * rank, 2 * ports), half),
            pltpu.VMEM((max(twos, 1), 2, 2, rank, rank), half),
            pltpu.VMEM((4 * rank, 2 * rank), half),
            pltpu.VMEM((max(twos, 1), 8 * rank, 2 * rank), half),
            pltpu.VMEM((stages + 1, 4, scen, 2 * rank), half),
            pltpu.VMEM((stages, 3, 4, scen, 2 * rank), half),
            pltpu.VMEM((4, scen, 2 * ports), jnp.float32),
            pltpu.VMEM((4, 2, scen, ports), half),
            pltpu.SemaphoreType.DMA((14,)),
            pltpu.SemaphoreType.DMA,
            pltpu.SemaphoreType.DMA((4,)),
            pltpu.SemaphoreType.DMA((4, SUB)),
            pltpu.SemaphoreType.DMA((2,)),
            pltpu.SemaphoreType.DMA((2, 4)),
            pltpu.SemaphoreType.DMA((stages, 3)),
            pltpu.SemaphoreType.DMA((stages, 4, SUB)),
            pltpu.SemaphoreType.DMA((max(twos, 1), 2)),
            pltpu.SemaphoreType.DMA((max(twos, 1), 2)),
            pltpu.SemaphoreType.DMA((4,)),
            pltpu.SemaphoreType.DMA((4,)),
            pltpu.SemaphoreType.DMA,
        ],
        compiler_params=pltpu.CompilerParams(collective_id=0, has_side_effects=True, vmem_limit_bytes=50 * 1024 * 1024),
        cost_estimate=pl.CostEstimate(flops=3 << 30, bytes_accessed=6 << 20, transcendentals=0),
    )(spectra, near_kernel, project_basis, level_self, level_partner, expand_basis)
    return jnp.transpose(voltages, (0, 2, 1, 3))


def solution(mesh):
    return jax.shard_map(
        local,
        mesh=mesh,
        in_specs=(
            P(None, "freq", None, "box"),
            P("freq", None, "box", None),
            P("freq", None, "box", None),
            P(None, "freq", None, "box", None),
            P(None, "freq", None, "box", None),
            P("freq", None, "box", None),
        ),
        out_specs=P(None, "freq", None, "box"),
        check_vma=False,
    )
```

```python
import functools

import jax
import jax.numpy as jnp
from jax import lax
from jax.experimental import pallas as pl
from jax.experimental.pallas import tpu as pltpu
from jax.sharding import PartitionSpec as P

HALO = 128
TILE = 256
SUB = 2
MESH = pl.DeviceIdType.MESH
STAGES = ((0, 1), (2,), (3, 4), (5, 6))
STEPS = (
    ("project", 0, 0), ("project", 0, 1), ("rims", 0), ("project", 1, 0),
    ("onward",), ("project", 1, 1), ("level", 0, 0, 0), ("project", 2, 0),
    ("rims", 1), ("level", 0, 0, 1), ("level", 0, 1, 0), ("level", 1, 0, 0),
    ("project", 3, 0), ("level", 1, 0, 1), ("project", 2, 1), ("level", 0, 1, 1),
    ("near", 0), ("rims", 2), ("level", 1, 1, 0), ("near", 1),
    ("project", 3, 1), ("level", 0, 2, 0), ("level", 0, 3, 0), ("rims", 3),
    ("level", 0, 2, 1), ("level", 2, 0, 0), ("level", 1, 1, 1), ("near", 2),
    ("level", 0, 3, 1), ("level", 2, 0, 1), ("level", 1, 2, 0), ("level", 2, 1, 0),
    ("level", 3, 0, 0), ("level", 1, 3, 0), ("level", 2, 1, 1), ("finish", 0, 0),
    ("level", 1, 2, 1), ("level", 2, 2, 0), ("level", 3, 1, 0), ("level", 2, 3, 0),
    ("finish", 1, 0), ("level", 1, 3, 1), ("level", 2, 2, 1), ("level", 3, 0, 1),
    ("level", 3, 2, 0), ("finish", 2, 0), ("level", 3, 1, 1), ("level", 2, 3, 1),
    ("finish", 0, 1), ("level", 3, 3, 0), ("level", 3, 2, 1), ("finish", 2, 1),
    ("finish", 1, 1), ("near", 3), ("finish", 3, 0), ("level", 3, 3, 1),
    ("finish", 3, 1),
)


def flip(index, stride):
    return index + stride - 2 * stride * ((index // stride) % 2)


def kernel(
    cur, near, proj, own, other, expand, out,
    spec, low_rim, high_rim, near_re, near_im, w_in, w_lev, w_out, far_raw, w_far, w_two, coef, part_in, near_sum, volt,
    load_sem, spec_sem, fwd_send, fwd_recv, rim_send, rim_recv, lev_send, lev_recv, far_send, far_recv, ret_send, ret_recv, home_sem,
):
    box, f = lax.axis_index("box"), lax.axis_index("freq")
    boxes = lax.axis_size("box")
    levels = own.shape[0]
    scen, ports = spec.shape[2], spec.shape[3]
    rank = proj.shape[-1]
    rows = scen // SUB
    up, down = lax.rem(box + 1, boxes), lax.rem(box + boxes - 1, boxes)
    peers = [f, flip(f, 1), flip(f, 2), flip(flip(f, 2), 1)]
    stages = len(STAGES)
    mates, pairs = [], []
    for stage in STAGES:
        first = flip(box, 1 << stage[0])
        if len(stage) == 2:
            mates.append([first, flip(box, 1 << stage[1]), flip(first, 1 << stage[1])])
            pairs.append(mates[-1][1])
        else:
            mates.append([first])
    everyone = [there for group in mates for there in group] + [up, down]

    barrier = pltpu.get_barrier_semaphore()
    for slot in (2, 3, 1):
        pl.semaphore_signal(barrier, inc=1, device_id={"freq": peers[slot]}, device_id_type=MESH)
    for there in everyone:
        pl.semaphore_signal(barrier, inc=1, device_id={"box": there}, device_id_type=MESH)

    own_copy = pltpu.make_async_copy(cur.at[f], spec.at[0], spec_sem)
    own_copy.start()
    loads = []

    def load(source, target):
        copy = pltpu.make_async_copy(source, target, load_sem.at[len(loads)])
        copy.start()
        loads.append(copy)

    load(proj.at[0, 0], w_in.at[0:ports, 0:rank])
    load(proj.at[0, 1], w_in.at[0:ports, rank : 2 * rank])
    load(proj.at[0, 0], w_in.at[ports : 2 * ports, rank : 2 * rank])
    for source, base in ((own, 0), (other, 2 * rank)):
        load(source.at[:, 0, 0], w_lev.at[:, base : base + rank, 0:rank])
        load(source.at[:, 0, 1], w_lev.at[:, base : base + rank, rank : 2 * rank])
        load(source.at[:, 0, 0], w_lev.at[:, base + rank : base + 2 * rank, rank : 2 * rank])
    width = near.shape[2]
    load(near.at[0, 0], near_re.at[0:width])
    load(near.at[0, 1], near_re.at[width : 2 * width])
    load(near.at[0, 1], near_im.at[0:width])
    load(near.at[0, 0], near_im.at[width : 2 * width])
    load(expand.at[0, 0], w_out.at[0:rank, 0:ports])
    load(expand.at[0, 1], w_out.at[0:rank, ports : 2 * ports])
    load(expand.at[0, 0], w_out.at[rank : 2 * rank, ports : 2 * ports])

    pl.semaphore_wait(barrier, 3 + len(everyone))

    def forward(slot, part):
        lines = pl.ds(part * rows, rows)
        return pltpu.make_async_remote_copy(
            src_ref=cur.at[peers[slot], :, lines],
            dst_ref=spec.at[slot, :, lines],
            send_sem=fwd_send.at[slot],
            recv_sem=fwd_recv.at[slot, part],
            device_id={"freq": peers[slot]},
            device_id_type=MESH,
        )

    def rim(slot, side):
        columns = pl.ds(ports - HALO, HALO) if side == 0 else pl.ds(0, HALO)
        return pltpu.make_async_remote_copy(
            src_ref=spec.at[slot, :, :, columns],
            dst_ref=(low_rim, high_rim)[side].at[slot],
            send_sem=rim_send.at[side],
            recv_sem=rim_recv.at[side, slot],
            device_id={"box": (up, down)[side]},
            device_id_type=MESH,
        )

    def exchange(stage, slot, part):
        lines = pl.ds(part * rows, rows)
        return [
            pltpu.make_async_remote_copy(
                src_ref=coef.at[stage, slot, lines],
                dst_ref=part_in.at[stage, place, slot, lines],
                send_sem=lev_send.at[stage, place],
                recv_sem=lev_recv.at[stage, slot, part],
                device_id={"box": there},
                device_id_type=MESH,
            )
            for place, there in enumerate(mates[stage])
        ]

    def landed(stage, slot, part):
        block = part_in.at[stage, pl.ds(0, len(mates[stage])), slot, pl.ds(part * rows, rows)]
        return pltpu.make_async_copy(block, block, lev_recv.at[stage, slot, part])

    def drained(ref, sem):
        pltpu.make_async_copy(ref, ref, sem).wait()

    twos = [stage for stage in range(stages) if len(STAGES[stage]) == 2]

    def factors(place):
        stage = STAGES[twos[place]]
        return [
            pltpu.make_async_remote_copy(
                src_ref=source.at[stage[0], 0],
                dst_ref=far_raw.at[place, which],
                send_sem=far_send.at[place, which],
                recv_sem=far_recv.at[place, which],
                device_id={"box": pairs[place]},
                device_id_type=MESH,
            )
            for which, source in enumerate((own, other))
        ]

    def give_back(slot, part):
        lines = pl.ds(part * rows, rows)
        return pltpu.make_async_remote_copy(
            src_ref=volt.at[slot, :, lines],
            dst_ref=out.at[f, :, lines],
            send_sem=ret_send.at[slot],
            recv_sem=ret_recv.at[slot],
            device_id={"freq": peers[slot]},
            device_id_type=MESH,
        )

    def home(part):
        lines = pl.ds(part * rows, rows)
        return pltpu.make_async_copy(volt.at[0, :, lines], out.at[f, :, lines], home_sem)

    for slot in (2, 3):
        forward(slot, 0).start()
    for part in range(SUB):
        forward(1, part).start()
    for place in range(len(twos)):
        for copy in factors(place):
            copy.start()

    def dot(left, right):
        return jnp.dot(left, right, preferred_element_type=jnp.float32)

    for copy in loads[:3]:
        copy.wait()
    w_in[ports : 2 * ports, 0:rank] = -w_in[0:ports, rank : 2 * rank]
    own_copy.wait()
    prepared = set()

    def prepare(what):
        if what in prepared:
            return
        prepared.add(what)
        if what == "level":
            for copy in loads[3:9]:
                copy.wait()
            for base in (0, 2 * rank):
                w_lev[:, base + rank : base + 2 * rank, 0:rank] = -w_lev[:, base : base + rank, rank : 2 * rank]
        elif isinstance(what, int):
            for copy in factors(what):
                copy.wait()
            low, high = STAGES[twos[what]]
            for which in range(2):
                top, real, imag = 2 * rank * which, far_raw[what, which, 0], far_raw[what, which, 1]
                w_far[top : top + rank, 0:rank] = real
                w_far[top : top + rank, rank : 2 * rank] = imag
                w_far[top + rank : top + 2 * rank, 0:rank] = -imag
                w_far[top + rank : top + 2 * rank, rank : 2 * rank] = real
            near_half = dot(w_lev[low], w_lev[high, 0 : 2 * rank])
            far_half = dot(w_far[...], w_lev[high, 2 * rank : 4 * rank])
            w_two[what, 0 : 4 * rank] = near_half.astype(jnp.bfloat16)
            w_two[what, 4 * rank : 8 * rank] = far_half.astype(jnp.bfloat16)
        elif what == "near":
            for copy in loads[9:13]:
                copy.wait()

            near_re[width : 2 * width] = -near_re[width : 2 * width]

            @pl.when(box == 0)
            def _():
                for weights in (near_re, near_im):
                    for top in (0, width):
                        weights[top : top + HALO] = jnp.zeros((HALO, ports), jnp.bfloat16)

            @pl.when(box == boxes - 1)
            def _():
                for weights in (near_re, near_im):
                    for end in (width, 2 * width):
                        weights[end - HALO : end] = jnp.zeros((HALO, ports), jnp.bfloat16)

        else:
            for copy in loads[13:16]:
                copy.wait()
            w_out[rank : 2 * rank, 0:ports] = -w_out[0:rank, ports : 2 * ports]

    for step in STEPS:
        kind = step[0]
        if kind == "project":
            slot, part = step[1:]
            lines = pl.ds(part * rows, rows)
            if slot != 0:
                forward(slot, part).wait_recv()
            total = dot(spec[slot, 0, lines], w_in[0:ports]) + dot(spec[slot, 1, lines], w_in[ports : 2 * ports])
            coef[0, slot, lines] = total.astype(jnp.bfloat16)
            for copy in exchange(0, slot, part):
                copy.start()
            prepare("level")
        elif kind == "onward":
            for part in range(1, SUB):
                for slot in (2, 3):
                    forward(slot, part).start()
        elif kind == "rims":
            for side in range(2):
                rim(step[1], side).start()
        elif kind == "level":
            stage, slot, part = step[1:]
            lines = pl.ds(part * rows, rows)
            if stage in twos:
                prepare(twos.index(stage))
                weights = w_two.at[twos.index(stage)]
            else:
                weights = w_lev.at[STAGES[stage][0]]
            landed(stage, slot, part).wait()
            blocks = [coef[stage, slot, lines]] + [part_in[stage, place, slot, lines] for place in range(len(mates[stage]))]
            total = dot(jnp.concatenate(blocks, axis=-1), weights[...])
            coef[stage + 1, slot, lines] = total.astype(jnp.bfloat16)
            if stage + 1 < stages:
                for copy in exchange(stage + 1, slot, part):
                    copy.start()
        elif kind == "near":
            prepare("near")
            prepare("out")
            slot = step[1]
            for side in range(2):
                rim(slot, side).wait_recv()
            bands = [band[slot, component] for component in range(2) for band in (low_rim, spec, high_rim)]
            window = jnp.concatenate(bands, axis=-1)
            for component, weights in enumerate((near_re, near_im)):
                for left in range(0, ports, TILE):
                    start = component * ports + left
                    near_sum[slot, :, start : start + TILE] = dot(window, weights[:, left : left + TILE])
        else:
            slot, part = step[1:]
            lines = pl.ds(part * rows, rows)
            final = coef[stages, slot, lines]
            for component in range(2):
                for left in range(0, ports, TILE):
                    columns = slice(component * ports + left, component * ports + left + TILE)
                    total = dot(final, w_out[:, columns]) + near_sum[slot, lines, columns]
                    volt[slot, component, lines, left : left + TILE] = total.astype(jnp.bfloat16)
            if slot == 0:
                home(part).start()
            else:
                give_back(slot, part).start()

    drained(low_rim, rim_send.at[0])
    drained(high_rim, rim_send.at[1])
    for stage in range(stages):
        for place in range(len(mates[stage])):
            drained(coef.at[stage], lev_send.at[stage, place])
    for slot in range(1, 4):
        drained(spec.at[slot], fwd_send.at[slot])
        drained(volt.at[slot], ret_send.at[slot])
        drained(out.at[peers[slot]], ret_recv.at[slot])
    drained(volt.at[0], home_sem)


def local(currents, near_kernel, project_basis, level_self, level_partner, expand_basis):
    spectra = jnp.transpose(currents, (0, 2, 1, 3))
    bins, _, scen, ports = spectra.shape
    levels, rank = level_self.shape[0], level_self.shape[-1]
    width = near_kernel.shape[2]
    half = jnp.bfloat16
    stages, twos = len(STAGES), sum(len(stage) == 2 for stage in STAGES)
    voltages = pl.pallas_call(
        kernel,
        out_shape=jax.ShapeDtypeStruct(spectra.shape, half),
        in_specs=[pl.BlockSpec(memory_space=pl.ANY)] * 6,
        out_specs=pl.BlockSpec(memory_space=pl.ANY),
        scratch_shapes=[
            pltpu.VMEM((4, 2, scen, ports), half),
            pltpu.VMEM((4, 2, scen, HALO), half),
            pltpu.VMEM((4, 2, scen, HALO), half),
            pltpu.VMEM((2 * width, ports), half),
            pltpu.VMEM((2 * width, ports), half),
            pltpu.VMEM((2 * ports, 2 * rank), half),
            pltpu.VMEM((levels, 4 * rank, 2 * rank), half),
            pltpu.VMEM((2 * rank, 2 * ports), half),
            pltpu.VMEM((max(twos, 1), 2, 2, rank, rank), half),
            pltpu.VMEM((4 * rank, 2 * rank), half),
            pltpu.VMEM((max(twos, 1), 8 * rank, 2 * rank), half),
            pltpu.VMEM((stages + 1, 4, scen, 2 * rank), half),
            pltpu.VMEM((stages, 3, 4, scen, 2 * rank), half),
            pltpu.VMEM((4, scen, 2 * ports), jnp.float32),
            pltpu.VMEM((4, 2, scen, ports), half),
            pltpu.SemaphoreType.DMA((16,)),
            pltpu.SemaphoreType.DMA,
            pltpu.SemaphoreType.DMA((4,)),
            pltpu.SemaphoreType.DMA((4, SUB)),
            pltpu.SemaphoreType.DMA((2,)),
            pltpu.SemaphoreType.DMA((2, 4)),
            pltpu.SemaphoreType.DMA((stages, 3)),
            pltpu.SemaphoreType.DMA((stages, 4, SUB)),
            pltpu.SemaphoreType.DMA((max(twos, 1), 2)),
            pltpu.SemaphoreType.DMA((max(twos, 1), 2)),
            pltpu.SemaphoreType.DMA((4,)),
            pltpu.SemaphoreType.DMA((4,)),
            pltpu.SemaphoreType.DMA,
        ],
        compiler_params=pltpu.CompilerParams(collective_id=0, has_side_effects=True, vmem_limit_bytes=50 * 1024 * 1024),
        cost_estimate=pl.CostEstimate(flops=3 << 30, bytes_accessed=6 << 20, transcendentals=0),
    )(spectra, near_kernel, project_basis, level_self, level_partner, expand_basis)
    return jnp.transpose(voltages, (0, 2, 1, 3))


def solution(mesh):
    return jax.shard_map(
        local,
        mesh=mesh,
        in_specs=(
            P(None, "freq", None, "box"),
            P("freq", None, "box", None),
            P("freq", None, "box", None),
            P(None, "freq", None, "box", None),
            P(None, "freq", None, "box", None),
            P("freq", None, "box", None),
        ),
        out_specs=P(None, "freq", None, "box"),
        check_vma=False,
    )
```

```python
import functools

import jax
import jax.numpy as jnp
from jax import lax
from jax.experimental import pallas as pl
from jax.experimental.pallas import tpu as pltpu
from jax.sharding import PartitionSpec as P

HALO = 128
TILE = 256
SUB = 1
MESH = pl.DeviceIdType.MESH
STAGES = ((0, 1), (2,), (3, 4), (5, 6))
STEPS = (
    ("project", 0, 0), ("project", 1, 0), ("level", 0, 0, 0), ("rims", 0),
    ("level", 1, 0, 0), ("rims", 1), ("level", 0, 1, 0), ("project", 2, 0),
    ("near", 1), ("project", 3, 0), ("factors",), ("level", 0, 2, 0), ("rims", 2),
    ("rims", 3), ("level", 1, 1, 0), ("level", 2, 0, 0), ("level", 0, 3, 0),
    ("near", 0), ("near", 3), ("level", 1, 2, 0), ("level", 2, 1, 0),
    ("level", 3, 0, 0), ("finish", 0, 0), ("level", 1, 3, 0), ("level", 2, 2, 0),
    ("near", 2), ("level", 2, 3, 0), ("level", 3, 2, 0), ("finish", 2, 0),
    ("level", 3, 1, 0), ("level", 3, 3, 0), ("finish", 3, 0), ("finish", 1, 0),
)


def flip(index, stride):
    return index + stride - 2 * stride * ((index // stride) % 2)


def kernel(
    cur, near, proj, own, other, expand, out,
    spec, low_rim, high_rim, near_re, near_im, w_in, w_lev, w_out, far_raw, w_far, w_two, coef, part_in, near_sum, volt,
    load_sem, spec_sem, fwd_send, fwd_recv, rim_send, rim_recv, lev_send, lev_recv, far_send, far_recv, ret_send, ret_recv, home_sem,
):
    box, f = lax.axis_index("box"), lax.axis_index("freq")
    boxes = lax.axis_size("box")
    levels = own.shape[0]
    scen, ports = spec.shape[2], spec.shape[3]
    rank = proj.shape[-1]
    rows = scen // SUB
    up, down = lax.rem(box + 1, boxes), lax.rem(box + boxes - 1, boxes)
    peers = [f, flip(f, 1), flip(f, 2), flip(flip(f, 2), 1)]
    stages = len(STAGES)
    mates, pairs = [], []
    for stage in STAGES:
        first = flip(box, 1 << stage[0])
        if len(stage) == 2:
            mates.append([first, flip(box, 1 << stage[1]), flip(first, 1 << stage[1])])
            pairs.append(mates[-1][1])
        else:
            mates.append([first])
    everyone = [there for group in mates for there in group] + [up, down]

    barrier = pltpu.get_barrier_semaphore()
    for slot in (2, 3, 1):
        pl.semaphore_signal(barrier, inc=1, device_id={"freq": peers[slot]}, device_id_type=MESH)
    for there in everyone:
        pl.semaphore_signal(barrier, inc=1, device_id={"box": there}, device_id_type=MESH)

    own_copy = pltpu.make_async_copy(cur.at[f], spec.at[0], spec_sem)
    own_copy.start()
    loads = []

    def load(source, target):
        copy = pltpu.make_async_copy(source, target, load_sem.at[len(loads)])
        copy.start()
        loads.append(copy)

    load(proj.at[0, 0], w_in.at[0:ports, 0:rank])
    load(proj.at[0, 1], w_in.at[0:ports, rank : 2 * rank])
    load(proj.at[0, 0], w_in.at[ports : 2 * ports, rank : 2 * rank])
    for source, base in ((own, 0), (other, 2 * rank)):
        load(source.at[:, 0, 0], w_lev.at[:, base : base + rank, 0:rank])
        load(source.at[:, 0, 1], w_lev.at[:, base : base + rank, rank : 2 * rank])
        load(source.at[:, 0, 0], w_lev.at[:, base + rank : base + 2 * rank, rank : 2 * rank])
    width = near.shape[2]
    load(near.at[0, 0], near_re.at[0:width])
    load(near.at[0, 1], near_re.at[width : 2 * width])
    load(near.at[0, 1], near_im.at[0:width])
    load(near.at[0, 0], near_im.at[width : 2 * width])
    load(expand.at[0, 0], w_out.at[0:rank, 0:ports])
    load(expand.at[0, 1], w_out.at[0:rank, ports : 2 * ports])
    load(expand.at[0, 0], w_out.at[rank : 2 * rank, ports : 2 * ports])

    pl.semaphore_wait(barrier, 3 + len(everyone))

    def forward(slot, part):
        lines = pl.ds(part * rows, rows)
        return pltpu.make_async_remote_copy(
            src_ref=cur.at[peers[slot], :, lines],
            dst_ref=spec.at[slot, :, lines],
            send_sem=fwd_send.at[slot],
            recv_sem=fwd_recv.at[slot, part],
            device_id={"freq": peers[slot]},
            device_id_type=MESH,
        )

    def rim(slot, side):
        columns = pl.ds(ports - HALO, HALO) if side == 0 else pl.ds(0, HALO)
        return pltpu.make_async_remote_copy(
            src_ref=spec.at[slot, :, :, columns],
            dst_ref=(low_rim, high_rim)[side].at[slot],
            send_sem=rim_send.at[side],
            recv_sem=rim_recv.at[side, slot],
            device_id={"box": (up, down)[side]},
            device_id_type=MESH,
        )

    def exchange(stage, slot, part):
        lines = pl.ds(part * rows, rows)
        return [
            pltpu.make_async_remote_copy(
                src_ref=coef.at[stage, slot, lines],
                dst_ref=part_in.at[stage, place, slot, lines],
                send_sem=lev_send.at[stage, place],
                recv_sem=lev_recv.at[stage, slot, part],
                device_id={"box": there},
                device_id_type=MESH,
            )
            for place, there in enumerate(mates[stage])
        ]

    def landed(stage, slot, part):
        block = part_in.at[stage, pl.ds(0, len(mates[stage])), slot, pl.ds(part * rows, rows)]
        return pltpu.make_async_copy(block, block, lev_recv.at[stage, slot, part])

    def drained(ref, sem):
        pltpu.make_async_copy(ref, ref, sem).wait()

    twos = [stage for stage in range(stages) if len(STAGES[stage]) == 2]

    def factors(place):
        stage = STAGES[twos[place]]
        return [
            pltpu.make_async_remote_copy(
                src_ref=source.at[stage[0], 0],
                dst_ref=far_raw.at[place, which],
                send_sem=far_send.at[place, which],
                recv_sem=far_recv.at[place, which],
                device_id={"box": pairs[place]},
                device_id_type=MESH,
            )
            for which, source in enumerate((own, other))
        ]

    def give_back(slot, part):
        lines = pl.ds(part * rows, rows)
        return pltpu.make_async_remote_copy(
            src_ref=volt.at[slot, :, lines],
            dst_ref=out.at[f, :, lines],
            send_sem=ret_send.at[slot],
            recv_sem=ret_recv.at[slot],
            device_id={"freq": peers[slot]},
            device_id_type=MESH,
        )

    def home(part):
        lines = pl.ds(part * rows, rows)
        return pltpu.make_async_copy(volt.at[0, :, lines], out.at[f, :, lines], home_sem)

    for slot in (2, 3):
        forward(slot, 0).start()
    for part in range(SUB):
        forward(1, part).start()
    for place in range(len(twos) - 1):
        for copy in factors(place):
            copy.start()

    def dot(left, right):
        return jnp.dot(left, right, preferred_element_type=jnp.float32)

    for copy in loads[:3]:
        copy.wait()
    w_in[ports : 2 * ports, 0:rank] = -w_in[0:ports, rank : 2 * rank]
    own_copy.wait()
    prepared = set()

    def prepare(what):
        if what in prepared:
            return
        prepared.add(what)
        if what == "level":
            for copy in loads[3:9]:
                copy.wait()
            for base in (0, 2 * rank):
                w_lev[:, base + rank : base + 2 * rank, 0:rank] = -w_lev[:, base : base + rank, rank : 2 * rank]
        elif isinstance(what, int):
            for copy in factors(what):
                copy.wait()
            low, high = STAGES[twos[what]]
            for which in range(2):
                top, real, imag = 2 * rank * which, far_raw[what, which, 0], far_raw[what, which, 1]
                w_far[top : top + rank, 0:rank] = real
                w_far[top : top + rank, rank : 2 * rank] = imag
                w_far[top + rank : top + 2 * rank, 0:rank] = -imag
                w_far[top + rank : top + 2 * rank, rank : 2 * rank] = real
            near_half = dot(w_lev[low], w_lev[high, 0 : 2 * rank])
            far_half = dot(w_far[...], w_lev[high, 2 * rank : 4 * rank])
            w_two[what, 0 : 4 * rank] = near_half.astype(jnp.bfloat16)
            w_two[what, 4 * rank : 8 * rank] = far_half.astype(jnp.bfloat16)
        elif what == "near":
            for copy in loads[9:13]:
                copy.wait()

            near_re[width : 2 * width] = -near_re[width : 2 * width]

            @pl.when(box == 0)
            def _():
                for weights in (near_re, near_im):
                    for top in (0, width):
                        weights[top : top + HALO] = jnp.zeros((HALO, ports), jnp.bfloat16)

            @pl.when(box == boxes - 1)
            def _():
                for weights in (near_re, near_im):
                    for end in (width, 2 * width):
                        weights[end - HALO : end] = jnp.zeros((HALO, ports), jnp.bfloat16)

        else:
            for copy in loads[13:16]:
                copy.wait()
            w_out[rank : 2 * rank, 0:ports] = -w_out[0:rank, ports : 2 * ports]

    for step in STEPS:
        kind = step[0]
        if kind == "project":
            slot, part = step[1:]
            lines = pl.ds(part * rows, rows)
            if slot != 0:
                forward(slot, part).wait_recv()
            total = dot(spec[slot, 0, lines], w_in[0:ports]) + dot(spec[slot, 1, lines], w_in[ports : 2 * ports])
            coef[0, slot, lines] = total.astype(jnp.bfloat16)
            for copy in exchange(0, slot, part):
                copy.start()
            prepare("level")
        elif kind == "onward":
            for part in range(1, SUB):
                for slot in (2, 3):
                    forward(slot, part).start()
        elif kind == "factors":
            for copy in factors(len(twos) - 1):
                copy.start()
        elif kind == "rims":
            for side in range(2):
                rim(step[1], side).start()
        elif kind == "level":
            stage, slot, part = step[1:]
            lines = pl.ds(part * rows, rows)
            if stage in twos:
                prepare(twos.index(stage))
                weights = w_two.at[twos.index(stage)]
            else:
                weights = w_lev.at[STAGES[stage][0]]
            landed(stage, slot, part).wait()
            blocks = [coef[stage, slot, lines]] + [part_in[stage, place, slot, lines] for place in range(len(mates[stage]))]
            total = dot(jnp.concatenate(blocks, axis=-1), weights[...])
            coef[stage + 1, slot, lines] = total.astype(jnp.bfloat16)
            if stage + 1 < stages:
                for copy in exchange(stage + 1, slot, part):
                    copy.start()
        elif kind == "near":
            prepare("near")
            prepare("out")
            slot = step[1]
            for side in range(2):
                rim(slot, side).wait_recv()
            bands = [band[slot, component] for component in range(2) for band in (low_rim, spec, high_rim)]
            window = jnp.concatenate(bands, axis=-1)
            for component, weights in enumerate((near_re, near_im)):
                for left in range(0, ports, TILE):
                    start = component * ports + left
                    near_sum[slot, :, start : start + TILE] = dot(window, weights[:, left : left + TILE])
        else:
            slot, part = step[1:]
            lines = pl.ds(part * rows, rows)
            final = coef[stages, slot, lines]
            for component in range(2):
                for left in range(0, ports, TILE):
                    columns = slice(component * ports + left, component * ports + left + TILE)
                    total = dot(final, w_out[:, columns]) + near_sum[slot, lines, columns]
                    volt[slot, component, lines, left : left + TILE] = total.astype(jnp.bfloat16)
            if slot == 0:
                home(part).start()
            else:
                give_back(slot, part).start()

    drained(low_rim, rim_send.at[0])
    drained(high_rim, rim_send.at[1])
    for stage in range(stages):
        for place in range(len(mates[stage])):
            drained(coef.at[stage], lev_send.at[stage, place])
    for slot in range(1, 4):
        drained(spec.at[slot], fwd_send.at[slot])
        drained(volt.at[slot], ret_send.at[slot])
        drained(out.at[peers[slot]], ret_recv.at[slot])
    drained(volt.at[0], home_sem)


def local(currents, near_kernel, project_basis, level_self, level_partner, expand_basis):
    spectra = jnp.transpose(currents, (0, 2, 1, 3))
    bins, _, scen, ports = spectra.shape
    levels, rank = level_self.shape[0], level_self.shape[-1]
    width = near_kernel.shape[2]
    half = jnp.bfloat16
    stages, twos = len(STAGES), sum(len(stage) == 2 for stage in STAGES)
    voltages = pl.pallas_call(
        kernel,
        out_shape=jax.ShapeDtypeStruct(spectra.shape, half),
        in_specs=[pl.BlockSpec(memory_space=pl.ANY)] * 6,
        out_specs=pl.BlockSpec(memory_space=pl.ANY),
        scratch_shapes=[
            pltpu.VMEM((4, 2, scen, ports), half),
            pltpu.VMEM((4, 2, scen, HALO), half),
            pltpu.VMEM((4, 2, scen, HALO), half),
            pltpu.VMEM((2 * width, ports), half),
            pltpu.VMEM((2 * width, ports), half),
            pltpu.VMEM((2 * ports, 2 * rank), half),
            pltpu.VMEM((levels, 4 * rank, 2 * rank), half),
            pltpu.VMEM((2 * rank, 2 * ports), half),
            pltpu.VMEM((max(twos, 1), 2, 2, rank, rank), half),
            pltpu.VMEM((4 * rank, 2 * rank), half),
            pltpu.VMEM((max(twos, 1), 8 * rank, 2 * rank), half),
            pltpu.VMEM((stages + 1, 4, scen, 2 * rank), half),
            pltpu.VMEM((stages, 3, 4, scen, 2 * rank), half),
            pltpu.VMEM((4, scen, 2 * ports), jnp.float32),
            pltpu.VMEM((4, 2, scen, ports), half),
            pltpu.SemaphoreType.DMA((16,)),
            pltpu.SemaphoreType.DMA,
            pltpu.SemaphoreType.DMA((4,)),
            pltpu.SemaphoreType.DMA((4, SUB)),
            pltpu.SemaphoreType.DMA((2,)),
            pltpu.SemaphoreType.DMA((2, 4)),
            pltpu.SemaphoreType.DMA((stages, 3)),
            pltpu.SemaphoreType.DMA((stages, 4, SUB)),
            pltpu.SemaphoreType.DMA((max(twos, 1), 2)),
            pltpu.SemaphoreType.DMA((max(twos, 1), 2)),
            pltpu.SemaphoreType.DMA((4,)),
            pltpu.SemaphoreType.DMA((4,)),
            pltpu.SemaphoreType.DMA,
        ],
        compiler_params=pltpu.CompilerParams(collective_id=0, has_side_effects=True, vmem_limit_bytes=50 * 1024 * 1024),
        cost_estimate=pl.CostEstimate(flops=3 << 30, bytes_accessed=6 << 20, transcendentals=0),
    )(spectra, near_kernel, project_basis, level_self, level_partner, expand_basis)
    return jnp.transpose(voltages, (0, 2, 1, 3))


def solution(mesh):
    return jax.shard_map(
        local,
        mesh=mesh,
        in_specs=(
            P(None, "freq", None, "box"),
            P("freq", None, "box", None),
            P("freq", None, "box", None),
            P(None, "freq", None, "box", None),
            P(None, "freq", None, "box", None),
            P("freq", None, "box", None),
        ),
        out_specs=P(None, "freq", None, "box"),
        check_vma=False,
    )
```

```python
import functools

import jax
import jax.numpy as jnp
from jax import lax
from jax.experimental import pallas as pl
from jax.experimental.pallas import tpu as pltpu
from jax.sharding import PartitionSpec as P

HALO = 128
TILE = 256
SUB = 1
MESH = pl.DeviceIdType.MESH
STAGES = ((0, 1), (2,), (3, 4), (5, 6))
STEPS = (
    ("project", 0, 0), ("project", 1, 0), ("onward",), ("level", 0, 0, 0), ("rims", 0),
    ("level", 1, 0, 0), ("rims", 1), ("level", 0, 1, 0), ("project", 2, 0),
    ("near", 1), ("project", 3, 0), ("factors",), ("level", 0, 2, 0), ("rims", 2),
    ("rims", 3), ("level", 1, 1, 0), ("level", 2, 0, 0), ("level", 0, 3, 0),
    ("near", 0), ("near", 3), ("level", 1, 2, 0), ("level", 2, 1, 0),
    ("level", 3, 0, 0), ("finish", 0, 0), ("level", 1, 3, 0), ("level", 2, 2, 0),
    ("near", 2), ("level", 2, 3, 0), ("level", 3, 2, 0), ("finish", 2, 0),
    ("level", 3, 1, 0), ("level", 3, 3, 0), ("finish", 3, 0), ("finish", 1, 0),
)


def flip(index, stride):
    return index + stride - 2 * stride * ((index // stride) % 2)


def kernel(
    cur, near, proj, own, other, expand, out,
    spec, low_rim, high_rim, near_re, near_im, w_in, w_lev, w_out, far_raw, w_far, w_two, coef, part_in, near_sum, volt,
    load_sem, spec_sem, fwd_send, fwd_recv, rim_send, rim_recv, lev_send, lev_recv, far_send, far_recv, ret_send, ret_recv, home_sem,
):
    box, f = lax.axis_index("box"), lax.axis_index("freq")
    boxes = lax.axis_size("box")
    levels = own.shape[0]
    scen, ports = spec.shape[2], spec.shape[3]
    rank = proj.shape[-1]
    rows = scen // SUB
    up, down = lax.rem(box + 1, boxes), lax.rem(box + boxes - 1, boxes)
    peers = [f, flip(f, 1), flip(f, 2), flip(flip(f, 2), 1)]
    stages = len(STAGES)
    mates, pairs = [], []
    for stage in STAGES:
        first = flip(box, 1 << stage[0])
        if len(stage) == 2:
            mates.append([first, flip(box, 1 << stage[1]), flip(first, 1 << stage[1])])
            pairs.append(mates[-1][1])
        else:
            mates.append([first])
    everyone = [there for group in mates for there in group] + [up, down]

    barrier = pltpu.get_barrier_semaphore()
    for slot in (2, 3, 1):
        pl.semaphore_signal(barrier, inc=1, device_id={"freq": peers[slot]}, device_id_type=MESH)
    for there in everyone:
        pl.semaphore_signal(barrier, inc=1, device_id={"box": there}, device_id_type=MESH)

    own_copy = pltpu.make_async_copy(cur.at[f], spec.at[0], spec_sem)
    own_copy.start()
    loads = []

    def load(source, target):
        copy = pltpu.make_async_copy(source, target, load_sem.at[len(loads)])
        copy.start()
        loads.append(copy)

    load(proj.at[0, 0], w_in.at[0:ports, 0:rank])
    load(proj.at[0, 1], w_in.at[0:ports, rank : 2 * rank])
    load(proj.at[0, 0], w_in.at[ports : 2 * ports, rank : 2 * rank])
    for source, base in ((own, 0), (other, 2 * rank)):
        load(source.at[:, 0, 0], w_lev.at[:, base : base + rank, 0:rank])
        load(source.at[:, 0, 1], w_lev.at[:, base : base + rank, rank : 2 * rank])
        load(source.at[:, 0, 0], w_lev.at[:, base + rank : base + 2 * rank, rank : 2 * rank])
    width = near.shape[2]
    load(near.at[0, 0], near_re.at[0:width])
    load(near.at[0, 1], near_re.at[width : 2 * width])
    load(near.at[0, 1], near_im.at[0:width])
    load(near.at[0, 0], near_im.at[width : 2 * width])
    load(expand.at[0, 0], w_out.at[0:rank, 0:ports])
    load(expand.at[0, 1], w_out.at[0:rank, ports : 2 * ports])
    load(expand.at[0, 0], w_out.at[rank : 2 * rank, ports : 2 * ports])

    pl.semaphore_wait(barrier, 3 + len(everyone))

    def forward(slot, part):
        lines = pl.ds(part * rows, rows)
        return pltpu.make_async_remote_copy(
            src_ref=cur.at[peers[slot], :, lines],
            dst_ref=spec.at[slot, :, lines],
            send_sem=fwd_send.at[slot],
            recv_sem=fwd_recv.at[slot, part],
            device_id={"freq": peers[slot]},
            device_id_type=MESH,
        )

    def rim(slot, side):
        columns = pl.ds(ports - HALO, HALO) if side == 0 else pl.ds(0, HALO)
        return pltpu.make_async_remote_copy(
            src_ref=spec.at[slot, :, :, columns],
            dst_ref=(low_rim, high_rim)[side].at[slot],
            send_sem=rim_send.at[side],
            recv_sem=rim_recv.at[side, slot],
            device_id={"box": (up, down)[side]},
            device_id_type=MESH,
        )

    def exchange(stage, slot, part):
        lines = pl.ds(part * rows, rows)
        return [
            pltpu.make_async_remote_copy(
                src_ref=coef.at[stage, slot, lines],
                dst_ref=part_in.at[stage, place, slot, lines],
                send_sem=lev_send.at[stage, place],
                recv_sem=lev_recv.at[stage, slot, part],
                device_id={"box": there},
                device_id_type=MESH,
            )
            for place, there in enumerate(mates[stage])
        ]

    def landed(stage, slot, part):
        block = part_in.at[stage, pl.ds(0, len(mates[stage])), slot, pl.ds(part * rows, rows)]
        return pltpu.make_async_copy(block, block, lev_recv.at[stage, slot, part])

    def drained(ref, sem):
        pltpu.make_async_copy(ref, ref, sem).wait()

    twos = [stage for stage in range(stages) if len(STAGES[stage]) == 2]

    def factors(place):
        stage = STAGES[twos[place]]
        return [
            pltpu.make_async_remote_copy(
                src_ref=source.at[stage[0], 0],
                dst_ref=far_raw.at[place, which],
                send_sem=far_send.at[place, which],
                recv_sem=far_recv.at[place, which],
                device_id={"box": pairs[place]},
                device_id_type=MESH,
            )
            for which, source in enumerate((own, other))
        ]

    def give_back(slot, part):
        lines = pl.ds(part * rows, rows)
        return pltpu.make_async_remote_copy(
            src_ref=volt.at[slot, :, lines],
            dst_ref=out.at[f, :, lines],
            send_sem=ret_send.at[slot],
            recv_sem=ret_recv.at[slot],
            device_id={"freq": peers[slot]},
            device_id_type=MESH,
        )

    def home(part):
        lines = pl.ds(part * rows, rows)
        return pltpu.make_async_copy(volt.at[0, :, lines], out.at[f, :, lines], home_sem)

    forward(2, 0).start()
    for part in range(SUB):
        forward(1, part).start()
    for place in range(len(twos) - 1):
        for copy in factors(place):
            copy.start()

    def dot(left, right):
        return jnp.dot(left, right, preferred_element_type=jnp.float32)

    for copy in loads[:3]:
        copy.wait()
    w_in[ports : 2 * ports, 0:rank] = -w_in[0:ports, rank : 2 * rank]
    own_copy.wait()
    prepared = set()

    def prepare(what):
        if what in prepared:
            return
        prepared.add(what)
        if what == "level":
            for copy in loads[3:9]:
                copy.wait()
            for base in (0, 2 * rank):
                w_lev[:, base + rank : base + 2 * rank, 0:rank] = -w_lev[:, base : base + rank, rank : 2 * rank]
        elif isinstance(what, int):
            for copy in factors(what):
                copy.wait()
            low, high = STAGES[twos[what]]
            for which in range(2):
                top, real, imag = 2 * rank * which, far_raw[what, which, 0], far_raw[what, which, 1]
                w_far[top : top + rank, 0:rank] = real
                w_far[top : top + rank, rank : 2 * rank] = imag
                w_far[top + rank : top + 2 * rank, 0:rank] = -imag
                w_far[top + rank : top + 2 * rank, rank : 2 * rank] = real
            near_half = dot(w_lev[low], w_lev[high, 0 : 2 * rank])
            far_half = dot(w_far[...], w_lev[high, 2 * rank : 4 * rank])
            w_two[what, 0 : 4 * rank] = near_half.astype(jnp.bfloat16)
            w_two[what, 4 * rank : 8 * rank] = far_half.astype(jnp.bfloat16)
        elif what == "near":
            for copy in loads[9:13]:
                copy.wait()

            near_re[width : 2 * width] = -near_re[width : 2 * width]

            @pl.when(box == 0)
            def _():
                for weights in (near_re, near_im):
                    for top in (0, width):
                        weights[top : top + HALO] = jnp.zeros((HALO, ports), jnp.bfloat16)

            @pl.when(box == boxes - 1)
            def _():
                for weights in (near_re, near_im):
                    for end in (width, 2 * width):
                        weights[end - HALO : end] = jnp.zeros((HALO, ports), jnp.bfloat16)

        else:
            for copy in loads[13:16]:
                copy.wait()
            w_out[rank : 2 * rank, 0:ports] = -w_out[0:rank, ports : 2 * ports]

    for step in STEPS:
        kind = step[0]
        if kind == "project":
            slot, part = step[1:]
            lines = pl.ds(part * rows, rows)
            if slot != 0:
                forward(slot, part).wait_recv()
            total = dot(spec[slot, 0, lines], w_in[0:ports]) + dot(spec[slot, 1, lines], w_in[ports : 2 * ports])
            coef[0, slot, lines] = total.astype(jnp.bfloat16)
            for copy in exchange(0, slot, part):
                copy.start()
            prepare("level")
        elif kind == "onward":
            forward(3, 0).start()
        elif kind == "factors":
            for copy in factors(len(twos) - 1):
                copy.start()
        elif kind == "rims":
            for side in range(2):
                rim(step[1], side).start()
        elif kind == "level":
            stage, slot, part = step[1:]
            lines = pl.ds(part * rows, rows)
            if stage in twos:
                prepare(twos.index(stage))
                weights = w_two.at[twos.index(stage)]
            else:
                weights = w_lev.at[STAGES[stage][0]]
            landed(stage, slot, part).wait()
            blocks = [coef[stage, slot, lines]] + [part_in[stage, place, slot, lines] for place in range(len(mates[stage]))]
            total = dot(jnp.concatenate(blocks, axis=-1), weights[...])
            coef[stage + 1, slot, lines] = total.astype(jnp.bfloat16)
            if stage + 1 < stages:
                for copy in exchange(stage + 1, slot, part):
                    copy.start()
        elif kind == "near":
            prepare("near")
            prepare("out")
            slot = step[1]
            for side in range(2):
                rim(slot, side).wait_recv()
            bands = [band[slot, component] for component in range(2) for band in (low_rim, spec, high_rim)]
            window = jnp.concatenate(bands, axis=-1)
            for component, weights in enumerate((near_re, near_im)):
                for left in range(0, ports, TILE):
                    start = component * ports + left
                    near_sum[slot, :, start : start + TILE] = dot(window, weights[:, left : left + TILE])
        else:
            slot, part = step[1:]
            lines = pl.ds(part * rows, rows)
            final = coef[stages, slot, lines]
            for component in range(2):
                for left in range(0, ports, TILE):
                    columns = slice(component * ports + left, component * ports + left + TILE)
                    total = dot(final, w_out[:, columns]) + near_sum[slot, lines, columns]
                    volt[slot, component, lines, left : left + TILE] = total.astype(jnp.bfloat16)
            if slot == 0:
                home(part).start()
            else:
                give_back(slot, part).start()

    drained(low_rim, rim_send.at[0])
    drained(high_rim, rim_send.at[1])
    for stage in range(stages):
        for place in range(len(mates[stage])):
            drained(coef.at[stage], lev_send.at[stage, place])
    for slot in range(1, 4):
        drained(spec.at[slot], fwd_send.at[slot])
        drained(volt.at[slot], ret_send.at[slot])
        drained(out.at[peers[slot]], ret_recv.at[slot])
    drained(volt.at[0], home_sem)


def local(currents, near_kernel, project_basis, level_self, level_partner, expand_basis):
    spectra = jnp.transpose(currents, (0, 2, 1, 3))
    bins, _, scen, ports = spectra.shape
    levels, rank = level_self.shape[0], level_self.shape[-1]
    width = near_kernel.shape[2]
    half = jnp.bfloat16
    stages, twos = len(STAGES), sum(len(stage) == 2 for stage in STAGES)
    voltages = pl.pallas_call(
        kernel,
        out_shape=jax.ShapeDtypeStruct(spectra.shape, half),
        in_specs=[pl.BlockSpec(memory_space=pl.ANY)] * 6,
        out_specs=pl.BlockSpec(memory_space=pl.ANY),
        scratch_shapes=[
            pltpu.VMEM((4, 2, scen, ports), half),
            pltpu.VMEM((4, 2, scen, HALO), half),
            pltpu.VMEM((4, 2, scen, HALO), half),
            pltpu.VMEM((2 * width, ports), half),
            pltpu.VMEM((2 * width, ports), half),
            pltpu.VMEM((2 * ports, 2 * rank), half),
            pltpu.VMEM((levels, 4 * rank, 2 * rank), half),
            pltpu.VMEM((2 * rank, 2 * ports), half),
            pltpu.VMEM((max(twos, 1), 2, 2, rank, rank), half),
            pltpu.VMEM((4 * rank, 2 * rank), half),
            pltpu.VMEM((max(twos, 1), 8 * rank, 2 * rank), half),
            pltpu.VMEM((stages + 1, 4, scen, 2 * rank), half),
            pltpu.VMEM((stages, 3, 4, scen, 2 * rank), half),
            pltpu.VMEM((4, scen, 2 * ports), jnp.float32),
            pltpu.VMEM((4, 2, scen, ports), half),
            pltpu.SemaphoreType.DMA((16,)),
            pltpu.SemaphoreType.DMA,
            pltpu.SemaphoreType.DMA((4,)),
            pltpu.SemaphoreType.DMA((4, SUB)),
            pltpu.SemaphoreType.DMA((2,)),
            pltpu.SemaphoreType.DMA((2, 4)),
            pltpu.SemaphoreType.DMA((stages, 3)),
            pltpu.SemaphoreType.DMA((stages, 4, SUB)),
            pltpu.SemaphoreType.DMA((max(twos, 1), 2)),
            pltpu.SemaphoreType.DMA((max(twos, 1), 2)),
            pltpu.SemaphoreType.DMA((4,)),
            pltpu.SemaphoreType.DMA((4,)),
            pltpu.SemaphoreType.DMA,
        ],
        compiler_params=pltpu.CompilerParams(collective_id=0, has_side_effects=True, vmem_limit_bytes=50 * 1024 * 1024),
        cost_estimate=pl.CostEstimate(flops=3 << 30, bytes_accessed=6 << 20, transcendentals=0),
    )(spectra, near_kernel, project_basis, level_self, level_partner, expand_basis)
    return jnp.transpose(voltages, (0, 2, 1, 3))


def solution(mesh):
    return jax.shard_map(
        local,
        mesh=mesh,
        in_specs=(
            P(None, "freq", None, "box"),
            P("freq", None, "box", None),
            P("freq", None, "box", None),
            P(None, "freq", None, "box", None),
            P(None, "freq", None, "box", None),
            P("freq", None, "box", None),
        ),
        out_specs=P(None, "freq", None, "box"),
        check_vma=False,
    )
```
